32 devices in a mesh: oi: 8 (over y, x, core), oj: 4 (over z).
Axes of the slice: x: 2, y: 2, z: 4, core: 2. Of those that a mesh axis runs over, the one named last changes fastest.
Arguments:
- amps: bfloat16 [64, 64, 4096], P('oi', 'oj'), may hold values from -6 to 6
- ladder_w: bfloat16 [2016, 2016], P('oj'), may hold values from -0.125 to 0.125
- fock: bfloat16 [64, 64], replicated, may hold values from -0.75 to 0.75
- eps_occ: float32 [64], replicated, may hold values from -2 to -0.3
- eps_pair: float32 [4096], replicated, may hold values from 0.5 to 4
Outputs:
- update: bfloat16 [64, 64, 4096], P('oi', 'oj')
The draws below stay inside these ranges and needn't reach their ends.
All inputs are finite; a program needn't handle non-finite values.
Results may differ from the reference program's by a relative error of at most 0.0054.
Values may be sent and summed in bfloat16 or wider, within the bound.
A program may use at most 128 MiB of HBM per device.

```python
import math
import jax
import jax.numpy as jnp
import numpy as np
from jax import lax

O = 64
NPAIR = 4096
PAIRS = 2016


def level_of(own_key, extent, cuts, low, largest):
    loudness = 1.0
    for axis_at, parts in cuts:
        steps = jax.random.uniform(jax.random.fold_in(jax.random.fold_in(own_key, 6), axis_at), (parts,), jnp.float32, low / len(cuts), largest / len(cuts))
        loudness = loudness * jnp.repeat(jnp.exp(steps), extent[axis_at] // parts).reshape((-1,) + (1,) * (len(extent) - 1 - axis_at))
    return loudness


def scatter_about(own_key, shape, scale, bound, cuts=(), kind=jnp.bfloat16):
    gain = level_of(own_key, shape, cuts, -0.22, 0.18) if cuts else 1.0
    array = jax.random.normal(own_key, shape, jnp.float32) * scale * gain
    return jnp.minimum(jnp.maximum(array, -bound), bound).astype(kind)


def setup_inputs(seed: int = 0) -> dict:
    arg_keys = jax.random.split(jax.random.key(seed), 6)
    return {
        "amps": scatter_about(arg_keys[0], (O, O, NPAIR), 1.0, 6.0, ((0, 8), (1, 4))),
        "ladder_w": scatter_about(arg_keys[1], (PAIRS, PAIRS), PAIRS ** -0.5, 0.125, ((0, 4),)),
        "fock": scatter_about(arg_keys[2], (O, O), O ** -0.5, 0.75),
        "eps_occ": jnp.clip(jax.random.uniform(arg_keys[3], (O,), jnp.float32, -2.0, -0.3), -2.0, -0.3),
        "eps_pair": jnp.clip(jax.random.uniform(arg_keys[4], (NPAIR,), jnp.float32, 0.5, 4.0), 0.5, 4.0),
    }


def pair_tables(occ):
    first, second = np.triu_indices(occ, 1)
    upper = (first * occ + second).astype(np.int32)
    lower = (second * occ + first).astype(np.int32)
    npairs = upper.shape[0]
    expand = np.full((occ * occ,), 2 * npairs, dtype=np.int32)
    expand[upper] = np.arange(npairs, dtype=np.int32)
    expand[lower] = npairs + np.arange(npairs, dtype=np.int32)
    return upper, lower, expand


def reference(amps, ladder_w, fock, eps_occ, eps_pair):
    upper, lower, expand = pair_tables(O)
    block = math.gcd(NPAIR, 4096)
    nblocks = NPAIR // block
    flat = amps.reshape(O * O, NPAIR)
    fock_wide = fock.astype(jnp.float32)

    def one_block(index):
        start = (index * block).astype(jnp.int32)
        cols = lax.dynamic_slice_in_dim(flat, start, block, 1)
        anti = (cols[upper].astype(jnp.float32) - cols[lower].astype(jnp.float32)).astype(jnp.bfloat16)
        ladder = jnp.dot(ladder_w.T, anti, preferred_element_type=jnp.float32)
        width = jnp.zeros((1, block), jnp.float32)
        full = jnp.concatenate([ladder, -ladder, width], axis=0)[expand].reshape(O, O, block)
        mixed = jnp.einsum("ikp,kj->ijp", cols.reshape(O, O, block).astype(jnp.float32), fock_wide)
        resid = (full - (mixed - jnp.transpose(mixed, (1, 0, 2)))).astype(jnp.bfloat16)
        resid = lax.optimization_barrier(resid)
        energies = lax.dynamic_slice_in_dim(eps_pair, start, block, 0)
        denom = energies[None, None, :] - eps_occ[:, None, None] - eps_occ[None, :, None]
        return (resid.astype(jnp.float32) / denom).astype(jnp.bfloat16)

    pieces = lax.map(one_block, jnp.arange(nblocks, dtype=jnp.int32))
    return jnp.transpose(pieces, (1, 2, 0, 3)).reshape(O, O, NPAIR)
```

```python
import functools

import jax
import jax.numpy as jnp
import numpy as np
from jax import lax
from jax.experimental import pallas as pl
from jax.experimental.pallas import tpu as pltpu
from jax.sharding import PartitionSpec as P

MESH = pl.DeviceIdType.MESH
LANES = 128
F32 = jnp.float32
BF16 = jnp.bfloat16


def pair_tables(occ):
    first, second = np.triu_indices(occ, 1)
    upper = (first * occ + second).astype(np.int32)
    lower = (second * occ + first).astype(np.int32)
    npairs = upper.shape[0]
    expand = np.full((occ * occ,), 2 * npairs, dtype=np.int32)
    expand[upper] = np.arange(npairs, dtype=np.int32)
    expand[lower] = npairs + np.arange(npairs, dtype=np.int32)
    return (upper, lower, expand)


def divide_out(resid, energies, first_eps, second_eps):
    denom = energies[None, None, :] - first_eps[:, None, None] - second_eps[None, :, None]
    held = lax.optimization_barrier(resid)
    return (held.astype(jnp.float32) / denom).astype(jnp.bfloat16)


def with_collectives(amps, ladder_w, fock, eps_occ, eps_pair):
    pair_amps = lax.all_to_all(
        lax.all_to_all(amps, "oi", split_axis=2, concat_axis=0, tiled=True),
        "oj",
        split_axis=2,
        concat_axis=1,
        tiled=True,
    )
    occ = pair_amps.shape[0]
    width = pair_amps.shape[2]
    upper, lower, expand = pair_tables(occ)
    flat = pair_amps.reshape(occ * occ, width)
    anti = (flat[upper].astype(jnp.float32) - flat[lower].astype(jnp.float32)).astype(jnp.bfloat16)
    contract = (((0,), (0,)), ((), ()))
    whole_w = lax.all_gather(ladder_w, "oj", axis=0, tiled=True)
    offset = (lax.axis_index("oi") * lax.axis_size("oj") + lax.axis_index("oj")) * width
    ladder = lax.dot_general(
        whole_w, anti[:, 0 : 0 + width], contract, preferred_element_type=jnp.float32
    )
    mixed = jnp.einsum("ikp,kj->ijp", pair_amps, fock, preferred_element_type=jnp.float32)
    filler = jnp.zeros((1, width), jnp.float32)
    full = jnp.concatenate([ladder, -ladder, filler], axis=0)[expand].reshape(occ, occ, width)
    resid = (full - (mixed - jnp.transpose(mixed, (1, 0, 2)))).astype(jnp.bfloat16)
    energies = lax.dynamic_slice_in_dim(eps_pair, offset + 0, width, 0)
    outgoing = divide_out(resid, energies, eps_occ, eps_occ).reshape(occ, occ, 1, 1, width)
    landed = lax.all_to_all(
        lax.all_to_all(outgoing, "oi", split_axis=0, concat_axis=2, tiled=True),
        "oj",
        split_axis=1,
        concat_axis=3,
        tiled=True,
    )
    rows_i = landed.shape[0]
    rows_j = landed.shape[1]
    arrived = landed.reshape(rows_i, rows_j, landed.shape[2] * landed.shape[3] * width)
    return arrived

def spot(first, second):
    return (first, second)


def greet_all(noi, noj):
    n = noi * noj
    me = lax.axis_index("oi") * noj + lax.axis_index("oj")
    barrier = pltpu.get_barrier_semaphore()

    @pl.loop(1, n)
    def _(t):
        peer = lax.rem(me + t, n)
        pl.semaphore_signal(
            barrier, inc=1, device_id=spot(peer // noj, lax.rem(peer, noj)), device_id_type=MESH
        )

    pl.semaphore_wait(barrier, n - 1)
    return me


def gather_kernel(noi, noj, amps, wpad, pair, wfull, asend, arecv, zsend, zrecv, xsend, xrecv,
                  csend, crecv, own):
    n = noi * noj
    bi, bj = amps.shape[0], amps.shape[1]
    nq = noi // 2
    rows = wpad.shape[0] // nq
    half = wpad.shape[1] // 2
    oi, oj = lax.axis_index("oi"), lax.axis_index("oj")
    q, core = oi // 2, lax.rem(oi, 2)
    me = greet_all(noi, noj)

    def part(ref, quarter, side):
        return ref.at[pl.ds(pl.multiple_of(quarter * rows, rows), rows),
                      pl.ds(pl.multiple_of(side * half, half), half)]

    def slot(shard, quarter, side):
        return part(wfull.at[shard], quarter, side)

    def z_copy(dz):
        return pltpu.make_async_remote_copy(
            src_ref=part(wpad, q, core), dst_ref=slot(oj, q, core),
            send_sem=zsend.at[dz], recv_sem=zrecv.at[dz],
            device_id=spot(oi, lax.rem(oj + dz, noj)), device_id_type=MESH)

    def x_copy(dz, dq):
        s = lax.rem(oj + noj - dz, noj)
        return pltpu.make_async_remote_copy(
            src_ref=slot(s, q, core), dst_ref=slot(s, q, core),
            send_sem=xsend.at[dz, dq], recv_sem=xrecv.at[dz, dq],
            device_id=spot(lax.rem(q + dq, nq) * 2 + core, oj), device_id_type=MESH)

    def c_copy(dz, dq):
        s = lax.rem(oj + noj - dz, noj)
        quarter = lax.rem(q + nq - dq, nq)
        return pltpu.make_async_remote_copy(
            src_ref=slot(s, quarter, core), dst_ref=slot(s, quarter, core),
            send_sem=csend.at[dz, dq], recv_sem=crecv.at[dz, dq],
            device_id=spot(q * 2 + 1 - core, oj), device_id_type=MESH)

    def a_copy(t):
        peer = lax.rem(me + t, n)
        return pltpu.make_async_remote_copy(
            src_ref=amps.at[:, :, pl.ds(pl.multiple_of(peer * LANES, LANES), LANES)],
            dst_ref=pair.at[pl.ds(oi * bi, bi), pl.ds(pl.multiple_of(oj * bj, bj), bj), :],
            send_sem=asend.at[t], recv_sem=arecv.at[t],
            device_id=spot(peer // noj, lax.rem(peer, noj)), device_id_type=MESH)

    for dz in range(1, noj):
        z_copy(dz).start()

    @pl.loop(1, n)
    def _(t):
        a_copy(t).start()

    mine = pltpu.make_async_copy(
        amps.at[:, :, pl.ds(pl.multiple_of(me * LANES, LANES), LANES)],
        pair.at[pl.ds(oi * bi, bi), pl.ds(pl.multiple_of(oj * bj, bj), bj), :], own.at[0])
    mine.start()
    whole = pltpu.make_async_copy(wpad, wfull.at[oj], own.at[1])
    whole.start()

    for dz in range(1, noj):
        z_copy(dz).wait_recv()
        for dq in range(1, nq):
            x_copy(dz, dq).start()
        c_copy(dz, 0).start()
    for dz in range(1, noj):
        for dq in range(1, nq):
            x_copy(dz, dq).wait_recv()
            c_copy(dz, dq).start()
    mine.wait()
    whole.wait()
    for dz in range(1, noj):
        z_copy(dz).wait_send()
        for dq in range(nq):
            if dq:
                x_copy(dz, dq).wait_send()
            c_copy(dz, dq).wait()

    @pl.loop(1, n)
    def _(t):
        a_copy(t).wait()


def gather(noi, noj, amps, wpad, occ):
    nq = noi // 2
    dma = pltpu.SemaphoreType.DMA
    return pl.pallas_call(
        functools.partial(gather_kernel, noi, noj),
        out_shape=(
            jax.ShapeDtypeStruct((occ, occ, LANES), BF16),
            jax.ShapeDtypeStruct((noj,) + wpad.shape, BF16),
        ),
        in_specs=[pl.BlockSpec(memory_space=pl.ANY)] * 2,
        out_specs=(pl.BlockSpec(memory_space=pl.ANY),) * 2,
        scratch_shapes=[
            dma((noi * noj,)), dma((noi * noj,)), dma((noj,)), dma((noj,)),
            dma((noj, nq)), dma((noj, nq)), dma((noj, nq)), dma((noj, nq)), dma((2,)),
        ],
        compiler_params=pltpu.CompilerParams(collective_id=0, has_side_effects=True),
    )(amps, wpad)


def spread_kernel(noi, noj, upd, out, send, recv, own):
    n = noi * noj
    bi, bj = out.shape[0], out.shape[1]
    me = greet_all(noi, noj)

    def block(peer):
        return upd.at[pl.ds((peer // noj) * bi, bi),
                      pl.ds(pl.multiple_of(lax.rem(peer, noj) * bj, bj), bj), :]

    here = out.at[:, :, pl.ds(pl.multiple_of(me * LANES, LANES), LANES)]

    def copy(t):
        peer = lax.rem(me + t, n)
        return pltpu.make_async_remote_copy(
            src_ref=block(peer), dst_ref=here, send_sem=send.at[t], recv_sem=recv.at[t],
            device_id=spot(peer // noj, lax.rem(peer, noj)), device_id_type=MESH)

    @pl.loop(1, n)
    def _(t):
        copy(t).start()

    mine = pltpu.make_async_copy(block(me), here, own)
    mine.start()
    mine.wait()

    @pl.loop(1, n)
    def _(t):
        copy(t).wait()


def spread(noi, noj, upd, bi, bj):
    dma = pltpu.SemaphoreType.DMA
    return pl.pallas_call(
        functools.partial(spread_kernel, noi, noj),
        out_shape=jax.ShapeDtypeStruct((bi, bj, noi * noj * LANES), BF16),
        in_specs=[pl.BlockSpec(memory_space=pl.ANY)],
        out_specs=pl.BlockSpec(memory_space=pl.ANY),
        scratch_shapes=[dma((noi * noj,)), dma((noi * noj,)), dma],
        compiler_params=pltpu.CompilerParams(collective_id=1, has_side_effects=True),
    )(upd)


def pair_start(occ, k):
    return k * (occ - 1) - k * (k - 1) // 2


def pack_anti(occ, shard, padded, wide, packed):
    nshards = packed.shape[0] // padded
    for s in range(nshards):
        packed[s * padded + shard:(s + 1) * padded, :] = jnp.zeros((padded - shard, LANES), F32)
    for k in range(occ - 1):
        row = wide[k * occ:(k + 1) * occ, :]
        col = wide[pl.ds(k, occ, stride=occ), :]
        diff = row - col
        at, end = pair_start(occ, k), pair_start(occ, k + 1)
        base = k + 1 - at
        while at < end:
            s = at // shard
            stop = min(end, (s + 1) * shard)
            lift = s * (padded - shard)
            packed[at + lift:stop + lift, :] = diff[at + base:stop + base, :]
            at = stop


def compute_kernel(occ, shard, padded, noj, pair, w, fock, eps_row, energies, upd, wide, mixed,
                   packed, lad, rf):
    me = lax.axis_index("oi") * noj + lax.axis_index("oj")
    flipped = fock[...].astype(F32).T.astype(BF16)

    @pl.loop(0, occ)
    def _(i):
        block = pair[i]
        at = pl.ds(pl.multiple_of(i * occ, occ), occ)
        wide[at, :] = block.astype(F32)
        mixed[at, :] = jnp.dot(flipped, block, preferred_element_type=F32)

    pack_anti(occ, shard, padded, wide, packed)
    left = packed[...].T.astype(BF16)
    step = 256
    for c in range(0, w.shape[1], step):
        lt = jnp.dot(left, w[:, c:c + step], preferred_element_type=F32)
        lad[c:c + step, :] = lt.T
    finish(occ, eps_row, energies[pl.ds(me, 1), :], lad, mixed, rf, upd)


def finish(occ, eps_row, energy, lad, mixed, rf, upd):
    for i in range(occ):
        if i == occ - 1:
            break
        row = mixed[i * occ:(i + 1) * occ, :]
        col = mixed[pl.ds(i, occ, stride=occ), :]
        at, n = pair_start(occ, i), occ - 1 - i
        diff = (row - col)[i + 1:, :]
        rf[i * occ + i + 1:(i + 1) * occ, :] = lad[at:at + n, :] - diff
    second = jnp.broadcast_to(eps_row[...], (LANES, LANES)).T[:occ, :]
    index = lax.broadcasted_iota(jnp.int32, (occ, LANES), 0)
    for i in range(occ):
        row = rf[i * occ:(i + 1) * occ, :]
        col = rf[pl.ds(i, occ, stride=occ), :]
        value = jnp.where(index > i, row, jnp.where(index < i, -col, 0.0))
        denom = (energy - eps_row[0:1, i:i + 1]) - second
        value = value.astype(BF16).astype(F32)
        upd[i] = (value / denom).astype(BF16)


def compute(noj, shard, padded, pair, w, fock, eps_row, energies):
    occ = pair.shape[0]
    vmem = pl.BlockSpec(memory_space=pltpu.VMEM)
    return pl.pallas_call(
        functools.partial(compute_kernel, occ, shard, padded, noj),
        out_shape=jax.ShapeDtypeStruct((occ, occ, LANES), BF16),
        in_specs=[vmem] * 5,
        out_specs=vmem,
        scratch_shapes=[
            pltpu.VMEM((occ * occ, LANES), F32), pltpu.VMEM((occ * occ, LANES), F32),
            pltpu.VMEM((w.shape[0], LANES), F32), pltpu.VMEM((w.shape[1], LANES), F32),
            pltpu.VMEM((occ * occ, LANES), F32),
        ],
        compiler_params=pltpu.CompilerParams(vmem_limit_bytes=40 * 2**20),
    )(pair, w, fock, eps_row, energies)


def up_to(value, unit):
    return -(-value // unit) * unit


def with_kernels(noi, noj, amps, ladder_w, fock, eps_occ, eps_pair):
    occ = amps.shape[0] * noi
    shard, cols = ladder_w.shape
    padded = up_to(shard, 16 * noi // 2)
    wpad = jnp.pad(ladder_w, ((0, padded - shard), (0, up_to(cols, 256) - cols)))
    pair, wfull = gather(noi, noj, amps, wpad, occ)
    eps_row = jnp.pad(eps_occ, (0, LANES - occ)).reshape(1, LANES)
    upd = compute(noj, shard, padded, pair, wfull.reshape(noj * padded, wpad.shape[1]), fock,
                  eps_row, eps_pair.reshape(noi * noj, LANES))
    return spread(noi, noj, upd, amps.shape[0], amps.shape[1])


def solution(mesh):
    noi, noj = mesh.shape["oi"], mesh.shape["oj"]

    def on_device(amps, *rest):
        fits = amps.shape[1] % 16 == 0 and amps.shape[2] == noi * noj * LANES
        fits = fits and noi % 2 == 0 and amps.shape[0] * noi <= LANES
        if fits:
            return with_kernels(noi, noj, amps, *rest)
        return with_collectives(amps, *rest)

    in_specs = (P("oi", "oj", None), P("oj", None), P(), P(), P())
    out_specs = P("oi", "oj", None)
    return jax.shard_map(
        on_device, mesh=mesh, in_specs=in_specs, out_specs=out_specs, check_vma=False
    )
```

```python
import functools

import jax
import jax.numpy as jnp
import numpy as np
from jax import lax
from jax.experimental import pallas as pl
from jax.experimental.pallas import tpu as pltpu
from jax.sharding import PartitionSpec as P

MESH = pl.DeviceIdType.MESH
LANES = 128
F32 = jnp.float32
BF16 = jnp.bfloat16


def pair_tables(occ):
    first, second = np.triu_indices(occ, 1)
    upper = (first * occ + second).astype(np.int32)
    lower = (second * occ + first).astype(np.int32)
    npairs = upper.shape[0]
    expand = np.full((occ * occ,), 2 * npairs, dtype=np.int32)
    expand[upper] = np.arange(npairs, dtype=np.int32)
    expand[lower] = npairs + np.arange(npairs, dtype=np.int32)
    return (upper, lower, expand)


def divide_out(resid, energies, first_eps, second_eps):
    denom = energies[None, None, :] - first_eps[:, None, None] - second_eps[None, :, None]
    held = lax.optimization_barrier(resid)
    return (held.astype(jnp.float32) / denom).astype(jnp.bfloat16)


def with_collectives(amps, ladder_w, fock, eps_occ, eps_pair):
    pair_amps = lax.all_to_all(
        lax.all_to_all(amps, "oi", split_axis=2, concat_axis=0, tiled=True),
        "oj",
        split_axis=2,
        concat_axis=1,
        tiled=True,
    )
    occ = pair_amps.shape[0]
    width = pair_amps.shape[2]
    upper, lower, expand = pair_tables(occ)
    flat = pair_amps.reshape(occ * occ, width)
    anti = (flat[upper].astype(jnp.float32) - flat[lower].astype(jnp.float32)).astype(jnp.bfloat16)
    contract = (((0,), (0,)), ((), ()))
    whole_w = lax.all_gather(ladder_w, "oj", axis=0, tiled=True)
    offset = (lax.axis_index("oi") * lax.axis_size("oj") + lax.axis_index("oj")) * width
    ladder = lax.dot_general(
        whole_w, anti[:, 0 : 0 + width], contract, preferred_element_type=jnp.float32
    )
    mixed = jnp.einsum("ikp,kj->ijp", pair_amps, fock, preferred_element_type=jnp.float32)
    filler = jnp.zeros((1, width), jnp.float32)
    full = jnp.concatenate([ladder, -ladder, filler], axis=0)[expand].reshape(occ, occ, width)
    resid = (full - (mixed - jnp.transpose(mixed, (1, 0, 2)))).astype(jnp.bfloat16)
    energies = lax.dynamic_slice_in_dim(eps_pair, offset + 0, width, 0)
    outgoing = divide_out(resid, energies, eps_occ, eps_occ).reshape(occ, occ, 1, 1, width)
    landed = lax.all_to_all(
        lax.all_to_all(outgoing, "oi", split_axis=0, concat_axis=2, tiled=True),
        "oj",
        split_axis=1,
        concat_axis=3,
        tiled=True,
    )
    rows_i = landed.shape[0]
    rows_j = landed.shape[1]
    arrived = landed.reshape(rows_i, rows_j, landed.shape[2] * landed.shape[3] * width)
    return arrived

def spot(first, second):
    return (first, second)


def greet_all(noi, noj):
    n = noi * noj
    me = lax.axis_index("oi") * noj + lax.axis_index("oj")
    barrier = pltpu.get_barrier_semaphore()

    @pl.loop(1, n)
    def _(t):
        peer = lax.rem(me + t, n)
        pl.semaphore_signal(
            barrier, inc=1, device_id=spot(peer // noj, lax.rem(peer, noj)), device_id_type=MESH
        )

    pl.semaphore_wait(barrier, n - 1)
    return me


def pair_start(occ, k):
    return k * (occ - 1) - k * (k - 1) // 2


def pack_anti(occ, shard, padded, wide, packed):
    nshards = packed.shape[0] // padded
    for s in range(nshards):
        packed[s * padded + shard:(s + 1) * padded, :] = jnp.zeros((padded - shard, LANES), F32)
    for k in range(occ - 1):
        row = wide[k * occ:(k + 1) * occ, :]
        col = wide[pl.ds(k, occ, stride=occ), :]
        diff = row - col
        at, end = pair_start(occ, k), pair_start(occ, k + 1)
        base = k + 1 - at
        while at < end:
            s = at // shard
            stop = min(end, (s + 1) * shard)
            lift = s * (padded - shard)
            packed[at + lift:stop + lift, :] = diff[at + base:stop + base, :]
            at = stop


def finish(occ, eps_row, energy, lad, mixed, rf, upd):
    for i in range(occ):
        if i == occ - 1:
            break
        row = mixed[i * occ:(i + 1) * occ, :]
        col = mixed[pl.ds(i, occ, stride=occ), :]
        at, n = pair_start(occ, i), occ - 1 - i
        diff = (row - col)[i + 1:, :]
        rf[i * occ + i + 1:(i + 1) * occ, :] = lad[at:at + n, :] - diff
    second = jnp.broadcast_to(eps_row[...], (LANES, LANES)).T[:occ, :]
    index = lax.broadcasted_iota(jnp.int32, (occ, LANES), 0)
    for i in range(occ):
        row = rf[i * occ:(i + 1) * occ, :]
        col = rf[pl.ds(i, occ, stride=occ), :]
        value = jnp.where(index > i, row, jnp.where(index < i, -col, 0.0))
        denom = (energy - eps_row[0:1, i:i + 1]) - second
        value = value.astype(BF16).astype(F32)
        upd[i] = (value / denom).astype(BF16)


def fused_kernel(noi, noj, shard, amps, wpad, fock, eps_row, energies, out, pair, wfull, wide, mixed,
                 packed, left, acc, lad, rf, upd, asend, arecv, zsend, zrecv, xsend, xrecv,
                 csend, crecv, osend, orecv, own):
    n = noi * noj
    bi, bj = amps.shape[0], amps.shape[1]
    occ = pair.shape[0]
    nq = noi // 2
    padded, cols = wpad.shape
    rows = padded // nq
    half = cols // 2
    oi, oj = lax.axis_index("oi"), lax.axis_index("oj")
    q, core = oi // 2, lax.rem(oi, 2)
    me = greet_all(noi, noj)

    def part(ref, quarter, side):
        return ref.at[pl.ds(pl.multiple_of(quarter * rows, rows), rows),
                      pl.ds(pl.multiple_of(side * half, half), half)]

    def slot(s, quarter, side):
        return part(wfull.at[s], quarter, side)

    def comes_from(d, h):
        return oj - h if d == 0 else oj + h

    def gets(d, h):
        return oj >= h if d == 0 else oj + h < noj

    def can_send(d, h):
        if d == 0:
            return jnp.logical_and(oj + 1 < noj, oj + 1 >= h)
        return jnp.logical_and(oj >= 1, oj + h - 1 < noj)

    def z_copy(d, h):
        s = oj - h + 1 if d == 0 else oj + h - 1
        return pltpu.make_async_remote_copy(
            src_ref=part(wpad, q, core) if h == 1 else slot(s, q, core),
            dst_ref=slot(s, q, core), send_sem=zsend.at[d, h], recv_sem=zrecv.at[d, h],
            device_id=spot(oi, oj + 1 if d == 0 else oj - 1), device_id_type=MESH)

    def x_copy(d, h, dq):
        s = comes_from(d, h)
        return pltpu.make_async_remote_copy(
            src_ref=slot(s, q, core), dst_ref=slot(s, q, core),
            send_sem=xsend.at[d, h, dq], recv_sem=xrecv.at[d, h, dq],
            device_id=spot(lax.rem(q + dq, nq) * 2 + core, oj), device_id_type=MESH)

    def c_copy(d, h, dq):
        s = comes_from(d, h)
        quarter = lax.rem(q + nq - dq, nq)
        return pltpu.make_async_remote_copy(
            src_ref=slot(s, quarter, core), dst_ref=slot(s, quarter, core),
            send_sem=csend.at[d, h, dq], recv_sem=crecv.at[d, h, dq],
            device_id=spot(q * 2 + 1 - core, oj), device_id_type=MESH)

    def target(peer):
        return spot(peer // noj, lax.rem(peer, noj))

    def columns(ref, peer):
        return ref.at[:, :, pl.ds(pl.multiple_of(peer * LANES, LANES), LANES)]

    def block(ref, peer):
        return ref.at[pl.ds((peer // noj) * bi, bi),
                      pl.ds(pl.multiple_of(lax.rem(peer, noj) * bj, bj), bj), :]

    def a_copy(t):
        peer = lax.rem(me + t, n)
        return pltpu.make_async_remote_copy(
            src_ref=columns(amps, peer), dst_ref=block(pair, me),
            send_sem=asend.at[t], recv_sem=arecv.at[t],
            device_id=target(peer), device_id_type=MESH)

    def o_copy(t):
        peer = lax.rem(me + t, n)
        return pltpu.make_async_remote_copy(
            src_ref=block(upd, peer), dst_ref=columns(out, me),
            send_sem=osend.at[t], recv_sem=orecv.at[t],
            device_id=target(peer), device_id_type=MESH)

    def z_start(d, h):
        @pl.when(can_send(d, h))
        def _():
            z_copy(d, h).start()

    for d in range(2):
        z_start(d, 1)

    @pl.loop(1, n)
    def _(t):
        a_copy(t).start()

    mine = pltpu.make_async_copy(columns(amps, me), block(pair, me), own.at[0])
    mine.start()
    whole = pltpu.make_async_copy(wpad, wfull.at[oj], own.at[1])
    whole.start()

    for h in range(1, noj):
        for d in range(2):
            @pl.when(gets(d, h))
            def _():
                z_copy(d, h).wait_recv()
            if h + 1 < noj:
                z_start(d, h + 1)

            @pl.when(gets(d, h))
            def _():
                for dq in range(1, nq):
                    x_copy(d, h, dq).start()
                c_copy(d, h, 0).start()

    def swap(h):
        for d in range(2):
            @pl.when(gets(d, h))
            def _():
                for dq in range(1, nq):
                    x_copy(d, h, dq).wait_recv()
                    c_copy(d, h, dq).start()

    def multiply(s, first):
        rows_of = left[:, pl.ds(pl.multiple_of(s * padded, padded), padded)]

        @pl.loop(0, cols // 256)
        def _(c):
            at = pl.ds(pl.multiple_of(c * 256, 256), 256)
            term = jnp.dot(rows_of, wfull[s, :, at], preferred_element_type=F32)
            if first:
                acc[:, at] = term
            else:
                acc[:, at] += term

    swap(1)
    mine.wait()

    @pl.loop(1, n)
    def _(t):
        a_copy(t).wait_recv()

    flipped = fock[...].astype(F32).T.astype(BF16)

    @pl.loop(0, occ)
    def _(i):
        rows_i = pair[i]
        at = pl.ds(pl.multiple_of(i * occ, occ), occ)
        wide[at, :] = rows_i.astype(F32)
        mixed[at, :] = jnp.dot(flipped, rows_i, preferred_element_type=F32)

    pack_anti(occ, shard, padded, wide, packed)
    left[...] = packed[...].T.astype(BF16)
    whole.wait()
    multiply(oj, True)
    for h in range(1, noj):
        if h > 1:
            swap(h)
        for d in range(2):
            @pl.when(gets(d, h))
            def _():
                for dq in range(nq):
                    c_copy(d, h, dq).wait_recv()
                multiply(comes_from(d, h), False)

    @pl.loop(0, cols // 256)
    def _(c):
        at = pl.ds(pl.multiple_of(c * 256, 256), 256)
        lad[at, :] = acc[:, at].T

    finish(occ, eps_row, energies[pl.ds(me, 1), :], lad, mixed, rf, upd)

    @pl.loop(1, n)
    def _(t):
        o_copy(t).start()

    last = pltpu.make_async_copy(block(upd, me), columns(out, me), own.at[2])
    last.start()

    for h in range(1, noj):
        for d in range(2):
            @pl.when(can_send(d, h))
            def _():
                z_copy(d, h).wait_send()

            @pl.when(gets(d, h))
            def _():
                for dq in range(nq):
                    if dq:
                        x_copy(d, h, dq).wait_send()
                    c_copy(d, h, dq).wait_send()
    last.wait()

    @pl.loop(1, n)
    def _(t):
        a_copy(t).wait_send()
        o_copy(t).wait()


def fused(noi, noj, shard, amps, wpad, fock, eps_row, energies):
    occ = amps.shape[0] * noi
    padded, cols = wpad.shape
    dma, vmem = pltpu.SemaphoreType.DMA, pltpu.VMEM
    line, plane = dma((2, noj)), dma((2, noj, noi // 2))
    square = vmem((occ * occ, LANES), F32)
    everyone = dma((noi * noj,))
    remote, local = pl.BlockSpec(memory_space=pl.ANY), pl.BlockSpec(memory_space=vmem)
    return pl.pallas_call(
        functools.partial(fused_kernel, noi, noj, shard),
        out_shape=jax.ShapeDtypeStruct(amps.shape, BF16),
        in_specs=[remote, remote, local, local, local],
        out_specs=remote,
        scratch_shapes=[
            vmem((occ, occ, LANES), BF16), vmem((noj, padded, cols), BF16), square, square,
            vmem((noj * padded, LANES), F32), vmem((LANES, noj * padded), BF16),
            vmem((LANES, cols), F32), vmem((cols, LANES), F32), square,
            vmem((occ, occ, LANES), BF16),
            everyone, everyone, line, line, plane, plane, plane, plane, everyone, everyone,
            dma((3,)),
        ],
        compiler_params=pltpu.CompilerParams(
            collective_id=0, has_side_effects=True, vmem_limit_bytes=48 * 2**20),
    )(amps, wpad, fock, eps_row, energies)


def up_to(value, unit):
    return -(-value // unit) * unit


def with_kernels(noi, noj, amps, ladder_w, fock, eps_occ, eps_pair):
    occ = amps.shape[0] * noi
    shard, cols = ladder_w.shape
    padded = up_to(shard, 16 * noi // 2)
    wpad = jnp.pad(ladder_w, ((0, padded - shard), (0, up_to(cols, 256) - cols)))
    eps_row = jnp.pad(eps_occ, (0, LANES - occ)).reshape(1, LANES)
    energies = eps_pair.reshape(noi * noj, LANES)
    return fused(noi, noj, shard, amps, wpad, fock, eps_row, energies)


def solution(mesh):
    noi, noj = mesh.shape["oi"], mesh.shape["oj"]

    def on_device(amps, *rest):
        fits = amps.shape[1] % 16 == 0 and amps.shape[2] == noi * noj * LANES
        fits = fits and noi % 2 == 0 and amps.shape[0] * noi <= LANES
        if fits:
            return with_kernels(noi, noj, amps, *rest)
        return with_collectives(amps, *rest)

    in_specs = (P("oi", "oj", None), P("oj", None), P(), P(), P())
    out_specs = P("oi", "oj", None)
    return jax.shard_map(
        on_device, mesh=mesh, in_specs=in_specs, out_specs=out_specs, check_vma=False
    )
```

```python
import functools

import jax
import jax.numpy as jnp
import numpy as np
from jax import lax
from jax.experimental import pallas as pl
from jax.experimental.pallas import tpu as pltpu
from jax.sharding import PartitionSpec as P

MESH = pl.DeviceIdType.MESH
LANES = 128
F32 = jnp.float32
BF16 = jnp.bfloat16


def pair_tables(occ):
    first, second = np.triu_indices(occ, 1)
    upper = (first * occ + second).astype(np.int32)
    lower = (second * occ + first).astype(np.int32)
    npairs = upper.shape[0]
    expand = np.full((occ * occ,), 2 * npairs, dtype=np.int32)
    expand[upper] = np.arange(npairs, dtype=np.int32)
    expand[lower] = npairs + np.arange(npairs, dtype=np.int32)
    return (upper, lower, expand)


def divide_out(resid, energies, first_eps, second_eps):
    denom = energies[None, None, :] - first_eps[:, None, None] - second_eps[None, :, None]
    held = lax.optimization_barrier(resid)
    return (held.astype(jnp.float32) / denom).astype(jnp.bfloat16)


def with_collectives(amps, ladder_w, fock, eps_occ, eps_pair):
    pair_amps = lax.all_to_all(
        lax.all_to_all(amps, "oi", split_axis=2, concat_axis=0, tiled=True),
        "oj",
        split_axis=2,
        concat_axis=1,
        tiled=True,
    )
    occ = pair_amps.shape[0]
    width = pair_amps.shape[2]
    upper, lower, expand = pair_tables(occ)
    flat = pair_amps.reshape(occ * occ, width)
    anti = (flat[upper].astype(jnp.float32) - flat[lower].astype(jnp.float32)).astype(jnp.bfloat16)
    contract = (((0,), (0,)), ((), ()))
    whole_w = lax.all_gather(ladder_w, "oj", axis=0, tiled=True)
    offset = (lax.axis_index("oi") * lax.axis_size("oj") + lax.axis_index("oj")) * width
    ladder = lax.dot_general(
        whole_w, anti[:, 0 : 0 + width], contract, preferred_element_type=jnp.float32
    )
    mixed = jnp.einsum("ikp,kj->ijp", pair_amps, fock, preferred_element_type=jnp.float32)
    filler = jnp.zeros((1, width), jnp.float32)
    full = jnp.concatenate([ladder, -ladder, filler], axis=0)[expand].reshape(occ, occ, width)
    resid = (full - (mixed - jnp.transpose(mixed, (1, 0, 2)))).astype(jnp.bfloat16)
    energies = lax.dynamic_slice_in_dim(eps_pair, offset + 0, width, 0)
    outgoing = divide_out(resid, energies, eps_occ, eps_occ).reshape(occ, occ, 1, 1, width)
    landed = lax.all_to_all(
        lax.all_to_all(outgoing, "oi", split_axis=0, concat_axis=2, tiled=True),
        "oj",
        split_axis=1,
        concat_axis=3,
        tiled=True,
    )
    rows_i = landed.shape[0]
    rows_j = landed.shape[1]
    arrived = landed.reshape(rows_i, rows_j, landed.shape[2] * landed.shape[3] * width)
    return arrived

def spot(first, second):
    return (first, second)


def greet_all(noi, noj):
    n = noi * noj
    me = lax.axis_index("oi") * noj + lax.axis_index("oj")
    barrier = pltpu.get_barrier_semaphore()

    @pl.loop(1, n)
    def _(t):
        peer = lax.rem(me + t, n)
        pl.semaphore_signal(
            barrier, inc=1, device_id=spot(peer // noj, lax.rem(peer, noj)), device_id_type=MESH
        )

    pl.semaphore_wait(barrier, n - 1)
    return me


def pair_start(occ, k):
    return k * (occ - 1) - k * (k - 1) // 2


def pack_anti(occ, shard, padded, wide, packed):
    nshards = packed.shape[0] // padded
    for s in range(nshards):
        packed[s * padded + shard:(s + 1) * padded, :] = jnp.zeros((padded - shard, LANES), F32)
    for k in range(occ - 1):
        row = wide[k * occ:(k + 1) * occ, :]
        col = wide[pl.ds(k, occ, stride=occ), :]
        diff = row - col
        at, end = pair_start(occ, k), pair_start(occ, k + 1)
        base = k + 1 - at
        while at < end:
            s = at // shard
            stop = min(end, (s + 1) * shard)
            lift = s * (padded - shard)
            packed[at + lift:stop + lift, :] = diff[at + base:stop + base, :]
            at = stop


def residual(occ, low, high, lad, mixed, rf):
    for i in range(low, high):
        row = mixed[i * occ:(i + 1) * occ, :]
        col = mixed[pl.ds(i, occ, stride=occ), :]
        at, n = pair_start(occ, i), occ - 1 - i
        diff = (row - col)[i + 1:, :]
        rf[i * occ + i + 1:(i + 1) * occ, :] = lad[at:at + n, :] - diff


def divide(occ, start, full, cut, eps_row, energy, rf, upd):
    second = jnp.broadcast_to(eps_row[...], (LANES, LANES)).T[:occ, :]
    index = lax.broadcasted_iota(jnp.int32, (occ, LANES), 0)
    for i in range(start, occ):
        low, high = (0, occ if i < full else cut) if start == 0 else (cut, occ)
        if low == high:
            continue
        denom = (energy - eps_row[0:1, i:i + 1]) - second[low:high, :]
        col = rf[pl.ds(low * occ + i, high - low, stride=occ), :]
        if high <= i:
            value = -col
        else:
            row = rf[i * occ + low:i * occ + high, :]
            at = index[low:high, :]
            value = jnp.where(at > i, row, jnp.where(at < i, -col, 0.0))
        value = value.astype(BF16).astype(F32)
        upd[i, low:high, :] = (value / denom).astype(BF16)


def fused_kernel(noi, noj, shard, amps, wpad, fock, eps_row, energies, out, pair, wfull, wide, mixed,
                 packed, left, acc, lad, rf, upd, asend, arecv, zsend, zrecv, xsend, xrecv,
                 csend, crecv, osend, orecv, own):
    n = noi * noj
    bi, bj = amps.shape[0], amps.shape[1]
    occ = pair.shape[0]
    nq = noi // 2
    padded, cols = wpad.shape
    rows = padded // nq
    half = cols // 2
    side_cols = half // 2
    oi, oj = lax.axis_index("oi"), lax.axis_index("oj")
    q, core = oi // 2, lax.rem(oi, 2)
    me = greet_all(noi, noj)

    def part(ref, quarter, side, p):
        at = pl.multiple_of(p * half + side * side_cols, side_cols)
        return ref.at[pl.ds(pl.multiple_of(quarter * rows, rows), rows), pl.ds(at, side_cols)]

    def slot(s, quarter, side, p):
        return part(wfull.at[s], quarter, side, p)

    def comes_from(d, h):
        return oj - h if d == 0 else oj + h

    def gets(d, h):
        return oj >= h if d == 0 else oj + h < noj

    def can_send(d, h):
        if d == 0:
            return jnp.logical_and(oj + 1 < noj, oj + 1 >= h)
        return jnp.logical_and(oj >= 1, oj + h - 1 < noj)

    def z_copy(p, d, h):
        s = oj - h + 1 if d == 0 else oj + h - 1
        return pltpu.make_async_remote_copy(
            src_ref=part(wpad, q, core, p) if h == 1 else slot(s, q, core, p),
            dst_ref=slot(s, q, core, p),
            send_sem=zsend.at[2 * p + d, h], recv_sem=zrecv.at[2 * p + d, h],
            device_id=spot(oi, oj + 1 if d == 0 else oj - 1), device_id_type=MESH)

    def x_copy(p, d, h, dq):
        ref = slot(comes_from(d, h), q, core, p)
        return pltpu.make_async_remote_copy(
            src_ref=ref, dst_ref=ref,
            send_sem=xsend.at[2 * p + d, h, dq], recv_sem=xrecv.at[2 * p + d, h, dq],
            device_id=spot(lax.rem(q + dq, nq) * 2 + core, oj), device_id_type=MESH)

    def c_copy(p, d, h, dq):
        ref = slot(comes_from(d, h), lax.rem(q + nq - dq, nq), core, p)
        return pltpu.make_async_remote_copy(
            src_ref=ref, dst_ref=ref,
            send_sem=csend.at[2 * p + d, h, dq], recv_sem=crecv.at[2 * p + d, h, dq],
            device_id=spot(q * 2 + 1 - core, oj), device_id_type=MESH)

    def target(peer):
        return spot(peer // noj, lax.rem(peer, noj))

    def columns(ref, peer):
        return ref.at[:, :, pl.ds(pl.multiple_of(peer * LANES, LANES), LANES)]

    def block(ref, peer):
        return ref.at[pl.ds((peer // noj) * bi, bi),
                      pl.ds(pl.multiple_of(lax.rem(peer, noj) * bj, bj), bj), :]

    def a_copy(t):
        peer = lax.rem(me + t, n)
        return pltpu.make_async_remote_copy(
            src_ref=columns(amps, peer), dst_ref=block(pair, me),
            send_sem=asend.at[t], recv_sem=arecv.at[t],
            device_id=target(peer), device_id_type=MESH)

    def o_copy(t):
        peer = lax.rem(me + t, n)
        return pltpu.make_async_remote_copy(
            src_ref=block(upd, peer), dst_ref=columns(out, me),
            send_sem=osend.at[t], recv_sem=orecv.at[t],
            device_id=target(peer), device_id_type=MESH)

    def z_start(p, d, h):
        @pl.when(can_send(d, h))
        def _():
            z_copy(p, d, h).start()

    for p in range(2):
        for d in range(2):
            z_start(p, d, 1)

    @pl.loop(1, n)
    def _(t):
        a_copy(t).start()

    mine = pltpu.make_async_copy(columns(amps, me), block(pair, me), own.at[0])
    mine.start()
    whole = pltpu.make_async_copy(wpad, wfull.at[oj], own.at[1])
    whole.start()

    def arrive(p, h):
        for d in range(2):
            @pl.when(gets(d, h))
            def _():
                z_copy(p, d, h).wait_recv()
            if h + 1 < noj:
                z_start(p, d, h + 1)

            @pl.when(gets(d, h))
            def _():
                for dq in range(1, nq):
                    x_copy(p, d, h, dq).start()
                c_copy(p, d, h, 0).start()

    def swap(p, h):
        for d in range(2):
            @pl.when(gets(d, h))
            def _():
                for dq in range(1, nq):
                    x_copy(p, d, h, dq).wait_recv()
                    c_copy(p, d, h, dq).start()

    def multiply(p, s, first):
        rows_of = left[:, pl.ds(pl.multiple_of(s * padded, padded), padded)]

        @pl.loop(p * half // 256, (p + 1) * half // 256)
        def _(c):
            at = pl.ds(pl.multiple_of(c * 256, 256), 256)
            term = jnp.dot(rows_of, wfull[s, :, at], preferred_element_type=F32)
            if first:
                acc[:, at] = term
            else:
                acc[:, at] += term

    def ladder(p):
        for h in range(1, noj):
            swap(p, h)
            for d in range(2):
                @pl.when(gets(d, h))
                def _():
                    for dq in range(nq):
                        c_copy(p, d, h, dq).wait_recv()
                    multiply(p, comes_from(d, h), False)

        @pl.loop(p * half // 256, (p + 1) * half // 256)
        def _(c):
            at = pl.ds(pl.multiple_of(c * 256, 256), 256)
            lad[at, :] = acc[:, at].T

    for h in range(1, noj):
        for p in range(2):
            arrive(p, h)
    mine.wait()

    @pl.loop(1, n)
    def _(t):
        a_copy(t).wait_recv()

    flipped = fock[...].astype(F32).T.astype(BF16)

    @pl.loop(0, occ)
    def _(i):
        rows_i = pair[i]
        at = pl.ds(pl.multiple_of(i * occ, occ), occ)
        wide[at, :] = rows_i.astype(F32)
        mixed[at, :] = jnp.dot(flipped, rows_i, preferred_element_type=F32)

    pack_anti(occ, shard, padded, wide, packed)
    left[...] = packed[...].T.astype(BF16)
    whole.wait()
    multiply(0, oj, True)
    multiply(1, oj, True)

    unit = max(bi, bj)
    early = max(e for e in range(0, occ, unit) if pair_start(occ, e) <= half)
    energy = energies[pl.ds(me, 1), :]

    def send(now):
        @pl.loop(1, n)
        def _(t):
            peer = lax.rem(me + t, n)
            soon = jnp.logical_or(peer // noj < early // bi, lax.rem(peer, noj) < early // bj)

            @pl.when(soon if now else jnp.logical_not(soon))
            def _():
                o_copy(t).start()

    ladder(0)
    residual(occ, 0, early, lad, mixed, rf)
    divide(occ, 0, early, early, eps_row, energy, rf, upd)
    send(True)
    ladder(1)
    residual(occ, early, occ - 1, lad, mixed, rf)
    divide(occ, early, 0, early, eps_row, energy, rf, upd)
    send(False)

    last = pltpu.make_async_copy(block(upd, me), columns(out, me), own.at[2])
    last.start()

    for p in range(2):
        for h in range(1, noj):
            for d in range(2):
                @pl.when(can_send(d, h))
                def _():
                    z_copy(p, d, h).wait_send()

                @pl.when(gets(d, h))
                def _():
                    for dq in range(nq):
                        if dq:
                            x_copy(p, d, h, dq).wait_send()
                        c_copy(p, d, h, dq).wait_send()
    last.wait()

    @pl.loop(1, n)
    def _(t):
        a_copy(t).wait_send()
        o_copy(t).wait()


def fused(noi, noj, shard, amps, wpad, fock, eps_row, energies):
    occ = amps.shape[0] * noi
    padded, cols = wpad.shape
    dma, vmem = pltpu.SemaphoreType.DMA, pltpu.VMEM
    line, plane = dma((4, noj)), dma((4, noj, noi // 2))
    square = vmem((occ * occ, LANES), F32)
    everyone = dma((noi * noj,))
    remote, local = pl.BlockSpec(memory_space=pl.ANY), pl.BlockSpec(memory_space=vmem)
    return pl.pallas_call(
        functools.partial(fused_kernel, noi, noj, shard),
        out_shape=jax.ShapeDtypeStruct(amps.shape, BF16),
        in_specs=[remote, remote, local, local, local],
        out_specs=remote,
        scratch_shapes=[
            vmem((occ, occ, LANES), BF16), vmem((noj, padded, cols), BF16), square, square,
            vmem((noj * padded, LANES), F32), vmem((LANES, noj * padded), BF16),
            vmem((LANES, cols), F32), vmem((cols, LANES), F32), square,
            vmem((occ, occ, LANES), BF16),
            everyone, everyone, line, line, plane, plane, plane, plane, everyone, everyone,
            dma((3,)),
        ],
        compiler_params=pltpu.CompilerParams(
            collective_id=0, has_side_effects=True, vmem_limit_bytes=48 * 2**20),
    )(amps, wpad, fock, eps_row, energies)


def up_to(value, unit):
    return -(-value // unit) * unit


def with_kernels(noi, noj, amps, ladder_w, fock, eps_occ, eps_pair):
    occ = amps.shape[0] * noi
    shard, cols = ladder_w.shape
    padded = up_to(shard, 16 * noi // 2)
    wpad = jnp.pad(ladder_w, ((0, padded - shard), (0, up_to(cols, 512) - cols)))
    eps_row = jnp.pad(eps_occ, (0, LANES - occ)).reshape(1, LANES)
    energies = eps_pair.reshape(noi * noj, LANES)
    return fused(noi, noj, shard, amps, wpad, fock, eps_row, energies)


def solution(mesh):
    noi, noj = mesh.shape["oi"], mesh.shape["oj"]

    def on_device(amps, *rest):
        fits = amps.shape[1] % 16 == 0 and amps.shape[2] == noi * noj * LANES
        fits = fits and noi % 2 == 0 and amps.shape[0] * noi <= LANES
        if fits:
            return with_kernels(noi, noj, amps, *rest)
        return with_collectives(amps, *rest)

    in_specs = (P("oi", "oj", None), P("oj", None), P(), P(), P())
    out_specs = P("oi", "oj", None)
    return jax.shard_map(
        on_device, mesh=mesh, in_specs=in_specs, out_specs=out_specs, check_vma=False
    )
```

```python
import functools

import jax
import jax.numpy as jnp
import numpy as np
from jax import lax
from jax.experimental import pallas as pl
from jax.experimental.pallas import tpu as pltpu
from jax.sharding import PartitionSpec as P

MESH = pl.DeviceIdType.MESH
LANES = 128
F32 = jnp.float32
BF16 = jnp.bfloat16


def pair_tables(occ):
    first, second = np.triu_indices(occ, 1)
    upper = (first * occ + second).astype(np.int32)
    lower = (second * occ + first).astype(np.int32)
    npairs = upper.shape[0]
    expand = np.full((occ * occ,), 2 * npairs, dtype=np.int32)
    expand[upper] = np.arange(npairs, dtype=np.int32)
    expand[lower] = npairs + np.arange(npairs, dtype=np.int32)
    return (upper, lower, expand)


def divide_out(resid, energies, first_eps, second_eps):
    denom = energies[None, None, :] - first_eps[:, None, None] - second_eps[None, :, None]
    held = lax.optimization_barrier(resid)
    return (held.astype(jnp.float32) / denom).astype(jnp.bfloat16)


def with_collectives(amps, ladder_w, fock, eps_occ, eps_pair):
    pair_amps = lax.all_to_all(
        lax.all_to_all(amps, "oi", split_axis=2, concat_axis=0, tiled=True),
        "oj",
        split_axis=2,
        concat_axis=1,
        tiled=True,
    )
    occ = pair_amps.shape[0]
    width = pair_amps.shape[2]
    upper, lower, expand = pair_tables(occ)
    flat = pair_amps.reshape(occ * occ, width)
    anti = (flat[upper].astype(jnp.float32) - flat[lower].astype(jnp.float32)).astype(jnp.bfloat16)
    contract = (((0,), (0,)), ((), ()))
    whole_w = lax.all_gather(ladder_w, "oj", axis=0, tiled=True)
    offset = (lax.axis_index("oi") * lax.axis_size("oj") + lax.axis_index("oj")) * width
    ladder = lax.dot_general(
        whole_w, anti[:, 0 : 0 + width], contract, preferred_element_type=jnp.float32
    )
    mixed = jnp.einsum("ikp,kj->ijp", pair_amps, fock, preferred_element_type=jnp.float32)
    filler = jnp.zeros((1, width), jnp.float32)
    full = jnp.concatenate([ladder, -ladder, filler], axis=0)[expand].reshape(occ, occ, width)
    resid = (full - (mixed - jnp.transpose(mixed, (1, 0, 2)))).astype(jnp.bfloat16)
    energies = lax.dynamic_slice_in_dim(eps_pair, offset + 0, width, 0)
    outgoing = divide_out(resid, energies, eps_occ, eps_occ).reshape(occ, occ, 1, 1, width)
    landed = lax.all_to_all(
        lax.all_to_all(outgoing, "oi", split_axis=0, concat_axis=2, tiled=True),
        "oj",
        split_axis=1,
        concat_axis=3,
        tiled=True,
    )
    rows_i = landed.shape[0]
    rows_j = landed.shape[1]
    arrived = landed.reshape(rows_i, rows_j, landed.shape[2] * landed.shape[3] * width)
    return arrived

def spot(first, second):
    return (first, second)


def greet_all(noi, noj):
    n = noi * noj
    me = lax.axis_index("oi") * noj + lax.axis_index("oj")
    barrier = pltpu.get_barrier_semaphore()

    @pl.loop(1, n)
    def _(t):
        peer = lax.rem(me + t, n)
        pl.semaphore_signal(
            barrier, inc=1, device_id=spot(peer // noj, lax.rem(peer, noj)), device_id_type=MESH
        )

    pl.semaphore_wait(barrier, n - 1)
    return me


def pair_start(occ, k):
    return k * (occ - 1) - k * (k - 1) // 2


def pack_anti(occ, shard, padded, wide, packed):
    nshards = packed.shape[0] // padded
    for s in range(nshards):
        packed[s * padded + shard:(s + 1) * padded, :] = jnp.zeros((padded - shard, LANES), F32)
    for k in range(occ - 1):
        row = wide[k * occ:(k + 1) * occ, :]
        col = wide[pl.ds(k, occ, stride=occ), :]
        diff = row - col
        at, end = pair_start(occ, k), pair_start(occ, k + 1)
        base = k + 1 - at
        while at < end:
            s = at // shard
            stop = min(end, (s + 1) * shard)
            lift = s * (padded - shard)
            packed[at + lift:stop + lift, :] = diff[at + base:stop + base, :]
            at = stop


def residual(occ, low, high, lad, mixed, rf):
    for i in range(low, high):
        row = mixed[i * occ:(i + 1) * occ, :]
        col = mixed[pl.ds(i, occ, stride=occ), :]
        at, n = pair_start(occ, i), occ - 1 - i
        diff = (row - col)[i + 1:, :]
        rf[i * occ + i + 1:(i + 1) * occ, :] = lad[at:at + n, :] - diff


def divide(occ, start, full, cut, eps_row, energy, rf, upd):
    second = jnp.broadcast_to(eps_row[...], (LANES, LANES)).T[:occ, :]
    index = lax.broadcasted_iota(jnp.int32, (occ, LANES), 0)
    for i in range(start, occ):
        low, high = (0, occ if i < full else cut) if start == 0 else (cut, occ)
        if low == high:
            continue
        denom = (energy - eps_row[0:1, i:i + 1]) - second[low:high, :]
        col = rf[pl.ds(low * occ + i, high - low, stride=occ), :]
        if high <= i:
            value = -col
        else:
            row = rf[i * occ + low:i * occ + high, :]
            at = index[low:high, :]
            value = jnp.where(at > i, row, jnp.where(at < i, -col, 0.0))
        value = value.astype(BF16).astype(F32)
        upd[i, low:high, :] = (value / denom).astype(BF16)


def fused_kernel(noi, noj, shard, amps, wpad, fock, eps_row, energies, out, pair, wfull, wide, mixed,
                 packed, left, acc, lad, rf, upd, asend, arecv, zsend, zrecv, xsend, xrecv,
                 csend, crecv, osend, orecv, own):
    n = noi * noj
    bi, bj = amps.shape[0], amps.shape[1]
    occ = pair.shape[0]
    nq = noi // 2
    padded, cols = wpad.shape
    rows = padded // nq
    half = cols // 2
    side_cols = half // 2
    oi, oj = lax.axis_index("oi"), lax.axis_index("oj")
    q, core = oi // 2, lax.rem(oi, 2)
    me = greet_all(noi, noj)

    def part(ref, quarter, side, p):
        at = pl.multiple_of(p * half + side * side_cols, side_cols)
        return ref.at[pl.ds(pl.multiple_of(quarter * rows, rows), rows), pl.ds(at, side_cols)]

    def slot(s, quarter, side, p):
        return part(wfull.at[s], quarter, side, p)

    def comes_from(d, h):
        return oj - h if d == 0 else oj + h

    def gets(d, h):
        return oj >= h if d == 0 else oj + h < noj

    def can_send(d, h):
        if d == 0:
            return jnp.logical_and(oj + 1 < noj, oj + 1 >= h)
        return jnp.logical_and(oj >= 1, oj + h - 1 < noj)

    def z_copy(p, d, h):
        s = oj - h + 1 if d == 0 else oj + h - 1
        return pltpu.make_async_remote_copy(
            src_ref=part(wpad, q, core, p) if h == 1 else slot(s, q, core, p),
            dst_ref=slot(s, q, core, p),
            send_sem=zsend.at[2 * p + d, h], recv_sem=zrecv.at[2 * p + d, h],
            device_id=spot(oi, oj + 1 if d == 0 else oj - 1), device_id_type=MESH)

    def x_copy(p, d, h, dq):
        ref = slot(comes_from(d, h), q, core, p)
        return pltpu.make_async_remote_copy(
            src_ref=ref, dst_ref=ref,
            send_sem=xsend.at[2 * p + d, h, dq], recv_sem=xrecv.at[2 * p + d, h, dq],
            device_id=spot(lax.rem(q + dq, nq) * 2 + core, oj), device_id_type=MESH)

    def c_copy(p, d, h, dq):
        ref = slot(comes_from(d, h), lax.rem(q + nq - dq, nq), core, p)
        return pltpu.make_async_remote_copy(
            src_ref=ref, dst_ref=ref,
            send_sem=csend.at[2 * p + d, h, dq], recv_sem=crecv.at[2 * p + d, h, dq],
            device_id=spot(q * 2 + 1 - core, oj), device_id_type=MESH)

    def target(peer):
        return spot(peer // noj, lax.rem(peer, noj))

    def columns(ref, peer):
        return ref.at[:, :, pl.ds(pl.multiple_of(peer * LANES, LANES), LANES)]

    def block(ref, peer):
        return ref.at[pl.ds((peer // noj) * bi, bi),
                      pl.ds(pl.multiple_of(lax.rem(peer, noj) * bj, bj), bj), :]

    def a_copy(t):
        peer = lax.rem(me + t, n)
        return pltpu.make_async_remote_copy(
            src_ref=columns(amps, peer), dst_ref=block(pair, me),
            send_sem=asend.at[t], recv_sem=arecv.at[t],
            device_id=target(peer), device_id_type=MESH)

    def o_copy(t):
        peer = lax.rem(me + t, n)
        return pltpu.make_async_remote_copy(
            src_ref=block(upd, peer), dst_ref=columns(out, me),
            send_sem=osend.at[t], recv_sem=orecv.at[t],
            device_id=target(peer), device_id_type=MESH)

    def z_start(p, d, h):
        @pl.when(can_send(d, h))
        def _():
            z_copy(p, d, h).start()

    for p in range(2):
        for d in range(2):
            z_start(p, d, 1)

    @pl.loop(1, n)
    def _(t):
        a_copy(t).start()

    mine = pltpu.make_async_copy(columns(amps, me), block(pair, me), own.at[0])
    mine.start()
    whole = pltpu.make_async_copy(wpad, wfull.at[oj], own.at[1])
    whole.start()

    def arrive(p, h):
        for d in range(2):
            @pl.when(gets(d, h))
            def _():
                z_copy(p, d, h).wait_recv()
            if h + 1 < noj:
                z_start(p, d, h + 1)

            @pl.when(gets(d, h))
            def _():
                for dq in range(1, nq):
                    x_copy(p, d, h, dq).start()
                c_copy(p, d, h, 0).start()

    def swap(p, h):
        for d in range(2):
            @pl.when(gets(d, h))
            def _():
                for dq in range(1, nq):
                    x_copy(p, d, h, dq).wait_recv()
                    c_copy(p, d, h, dq).start()

    def multiply(p, s, first):
        rows_of = left[:, pl.ds(pl.multiple_of(s * padded, padded), padded)]

        @pl.loop(p * half // 256, (p + 1) * half // 256)
        def _(c):
            at = pl.ds(pl.multiple_of(c * 256, 256), 256)
            term = jnp.dot(rows_of, wfull[s, :, at], preferred_element_type=F32)
            if first:
                acc[:, at] = term
            else:
                acc[:, at] += term

    def ladder(p):
        for h in range(1, noj):
            swap(p, h)
            for d in range(2):
                @pl.when(gets(d, h))
                def _():
                    for dq in range(nq):
                        c_copy(p, d, h, dq).wait_recv()
                    multiply(p, comes_from(d, h), False)

        @pl.loop(p * half // 256, (p + 1) * half // 256)
        def _(c):
            at = pl.ds(pl.multiple_of(c * 256, 256), 256)
            lad[at, :] = acc[:, at].T

    for h in range(1, noj):
        for p in range(2):
            arrive(p, h)
    mine.wait()

    @pl.loop(1, n)
    def _(t):
        a_copy(t).wait_recv()

    flipped = fock[...].astype(F32).T.astype(BF16)

    @pl.loop(0, occ)
    def _(i):
        rows_i = pair[i]
        at = pl.ds(pl.multiple_of(i * occ, occ), occ)
        wide[at, :] = rows_i.astype(F32)
        mixed[at, :] = jnp.dot(flipped, rows_i, preferred_element_type=F32)

    pack_anti(occ, shard, padded, wide, packed)
    left[...] = packed[...].T.astype(BF16)
    whole.wait()
    multiply(0, oj, True)

    unit = max(bi, bj)
    early = max(e for e in range(0, occ, unit) if pair_start(occ, e) <= half)
    energy = energies[pl.ds(me, 1), :]

    def send(now):
        @pl.loop(1, n)
        def _(t):
            peer = lax.rem(me + t, n)
            soon = jnp.logical_or(peer // noj < early // bi, lax.rem(peer, noj) < early // bj)

            @pl.when(soon if now else jnp.logical_not(soon))
            def _():
                o_copy(t).start()

    ladder(0)
    residual(occ, 0, early, lad, mixed, rf)
    divide(occ, 0, early, early, eps_row, energy, rf, upd)
    send(True)
    multiply(1, oj, True)
    ladder(1)
    residual(occ, early, occ - 1, lad, mixed, rf)
    divide(occ, early, 0, early, eps_row, energy, rf, upd)
    send(False)

    last = pltpu.make_async_copy(block(upd, me), columns(out, me), own.at[2])
    last.start()

    for p in range(2):
        for h in range(1, noj):
            for d in range(2):
                @pl.when(can_send(d, h))
                def _():
                    z_copy(p, d, h).wait_send()

                @pl.when(gets(d, h))
                def _():
                    for dq in range(nq):
                        if dq:
                            x_copy(p, d, h, dq).wait_send()
                        c_copy(p, d, h, dq).wait_send()
    last.wait()

    @pl.loop(1, n)
    def _(t):
        a_copy(t).wait_send()
        o_copy(t).wait()


def fused(noi, noj, shard, amps, wpad, fock, eps_row, energies):
    occ = amps.shape[0] * noi
    padded, cols = wpad.shape
    dma, vmem = pltpu.SemaphoreType.DMA, pltpu.VMEM
    line, plane = dma((4, noj)), dma((4, noj, noi // 2))
    square = vmem((occ * occ, LANES), F32)
    everyone = dma((noi * noj,))
    remote, local = pl.BlockSpec(memory_space=pl.ANY), pl.BlockSpec(memory_space=vmem)
    return pl.pallas_call(
        functools.partial(fused_kernel, noi, noj, shard),
        out_shape=jax.ShapeDtypeStruct(amps.shape, BF16),
        in_specs=[remote, remote, local, local, local],
        out_specs=remote,
        scratch_shapes=[
            vmem((occ, occ, LANES), BF16), vmem((noj, padded, cols), BF16), square, square,
            vmem((noj * padded, LANES), F32), vmem((LANES, noj * padded), BF16),
            vmem((LANES, cols), F32), vmem((cols, LANES), F32), square,
            vmem((occ, occ, LANES), BF16),
            everyone, everyone, line, line, plane, plane, plane, plane, everyone, everyone,
            dma((3,)),
        ],
        compiler_params=pltpu.CompilerParams(
            collective_id=0, has_side_effects=True, vmem_limit_bytes=48 * 2**20),
    )(amps, wpad, fock, eps_row, energies)


def up_to(value, unit):
    return -(-value // unit) * unit


def with_kernels(noi, noj, amps, ladder_w, fock, eps_occ, eps_pair):
    occ = amps.shape[0] * noi
    shard, cols = ladder_w.shape
    padded = up_to(shard, 16 * noi // 2)
    wpad = jnp.pad(ladder_w, ((0, padded - shard), (0, up_to(cols, 512) - cols)))
    eps_row = jnp.pad(eps_occ, (0, LANES - occ)).reshape(1, LANES)
    energies = eps_pair.reshape(noi * noj, LANES)
    return fused(noi, noj, shard, amps, wpad, fock, eps_row, energies)


def solution(mesh):
    noi, noj = mesh.shape["oi"], mesh.shape["oj"]

    def on_device(amps, *rest):
        fits = amps.shape[1] % 16 == 0 and amps.shape[2] == noi * noj * LANES
        fits = fits and noi % 2 == 0 and amps.shape[0] * noi <= LANES
        if fits:
            return with_kernels(noi, noj, amps, *rest)
        return with_collectives(amps, *rest)

    in_specs = (P("oi", "oj", None), P("oj", None), P(), P(), P())
    out_specs = P("oi", "oj", None)
    return jax.shard_map(
        on_device, mesh=mesh, in_specs=in_specs, out_specs=out_specs, check_vma=False
    )
```
